32 devices in a mesh: samp: 16 (over z, y, x), pos: 2 (over core).
Axes of the slice: x: 2, y: 2, z: 4, core: 2. Of those that a mesh axis runs over, the one named last changes fastest.
Arguments:
- dosages: bfloat16 [32768, 4096], P('samp', 'pos')
- phenotypes: bfloat16 [32768, 2048], P('samp')
- gene_weights: bfloat16 [4096, 16], P('pos'), may hold values from -0.1875 to 0.1875
- gene_start: int32 [16], replicated, may hold values from 0 to 3072, as said below
- gene_end: int32 [16], replicated, may hold values from 1024 to 4096, as said below
Outputs:
- variant_z: float32 [2048, 4096], P('samp', 'pos')
- gene_z: float32 [2048, 16], P('samp', 'pos')
The draws below stay inside these ranges and needn't reach their ends.
Inputs may be any that keep to these rules, and one draw needn't show every extreme that they name: gene_end - gene_start lies between 1024 and 2048; some window starts at 0 and some ends at 4096. gene_end is greater than gene_start of the same gene.
All inputs are finite; a program needn't handle non-finite values.
Results may differ from the reference program's by a relative error of at most 0.0029.
Values sent between devices are 32-bit elements; how exact they have to be, the bound alone decides.
A program may use at most 128 MiB of HBM per device.

```python
import jax
import jax.numpy as jnp
from jax import lax

VARIANTS = 4096
GENES = 16
TRAITS = 2048
SAMPLES = 32768


def scaled_rows(key, columns):
    rows = jnp.arange(SAMPLES, dtype=jnp.float32)
    rising = 1.0 + 2.0 * rows / SAMPLES
    base = jax.random.normal(key, (SAMPLES, columns), jnp.float32)
    return (base * rising[:, None]).astype(jnp.bfloat16)


def draw_dosages(key, part):
    return scaled_rows(jax.random.fold_in(key, 3), VARIANTS)


def draw_phenotypes(key, part):
    return scaled_rows(jax.random.fold_in(key, 5), TRAITS)


def window_pair(key):
    first_key, second_key = jax.random.split(jax.random.fold_in(key, 11))
    length = jax.random.randint(first_key, (GENES,), VARIANTS // 4, VARIANTS // 2 + 1)
    length = length.at[0].set(VARIANTS // 4)
    length = length.at[1].set(VARIANTS // 4)
    length = length.at[2].set(VARIANTS // 2)
    begin = jax.random.randint(second_key, (GENES,), 0, VARIANTS - length + 1)
    begin = begin.at[0].set(0)
    begin = begin.at[1].set(VARIANTS - length[1])
    return (begin.astype(jnp.int32), (begin + length).astype(jnp.int32))


def draw_gene_start(key, part):
    return window_pair(key)[0]


def draw_gene_end(key, part):
    return window_pair(key)[1]


def steps_of(own_key, extent, cuts, least, largest):
    level = 1.0
    for axis_at, blocks in cuts:
        draws = jax.random.uniform(jax.random.fold_in(jax.random.fold_in(own_key, 6), axis_at), (blocks,), jnp.float32, least / len(cuts), largest / len(cuts))
        level = level * jnp.repeat(jnp.exp(draws), extent[axis_at] // blocks).reshape((-1,) + (1,) * (len(extent) - 1 - axis_at))
    return level


def normal_values(own_key, shape, scale, bound, shards=(), kind=jnp.bfloat16):
    loudness = steps_of(own_key, shape, shards, -0.22, 0.18) if shards else 1.0
    result = jax.random.normal(own_key, shape, jnp.float32) * scale * loudness
    return jnp.minimum(jnp.maximum(result, -bound), bound).astype(kind)


def setup_inputs(seed: int = 0) -> dict:
    streams_of = jax.random.split(jax.random.key(seed), 6)
    return {
        "dosages": draw_dosages(jax.random.fold_in(streams_of[5], 71), 0),
        "phenotypes": draw_phenotypes(jax.random.fold_in(streams_of[5], 71), 0),
        "gene_weights": normal_values(streams_of[2], (VARIANTS, GENES), (VARIANTS // 4) ** -0.5, 0.1875, ((0, 2),)),
        "gene_start": draw_gene_start(jax.random.fold_in(streams_of[5], 71), 0),
        "gene_end": draw_gene_end(jax.random.fold_in(streams_of[5], 71), 0),
    }


EPSILON = 1e-06

def contract(left, right):
    return lax.dot_general(left, right, (((0,), (0,)), ((), ())), preferred_element_type=jnp.float32)

def reference(dosages, phenotypes, gene_weights, gene_start, gene_end):
    position = jnp.arange(VARIANTS, dtype=jnp.int32)[:, None]
    inside = (position >= gene_start[None, :]) & (position < gene_end[None, :])
    masked = jnp.where(inside, gene_weights, jnp.zeros_like(gene_weights))
    predicted = jnp.dot(dosages, masked, preferred_element_type=jnp.float32)
    pred_low = predicted.astype(jnp.bfloat16)
    marginal = contract(phenotypes, dosages)
    gene_cross = contract(phenotypes, pred_low)
    mean_dose = lax.optimization_barrier(jnp.sum(jnp.square(dosages.astype(jnp.float32)), axis=0)) / SAMPLES
    mean_trait = lax.optimization_barrier(jnp.sum(jnp.square(phenotypes.astype(jnp.float32)), axis=0)) / SAMPLES
    mean_pred = lax.optimization_barrier(jnp.sum(predicted * predicted, axis=0)) / SAMPLES
    variant_z = marginal / jnp.sqrt(SAMPLES * (mean_trait[:, None] + EPSILON) * (mean_dose[None, :] + EPSILON))
    gene_z = gene_cross / jnp.sqrt(SAMPLES * (mean_trait[:, None] + EPSILON) * (mean_pred[None, :] + EPSILON))
    return (variant_z, gene_z)
```

```python
import functools

import jax
import jax.numpy as jnp
from jax import lax
from jax.experimental import pallas as pl
from jax.experimental.pallas import tpu as pltpu
from jax.sharding import PartitionSpec as P

EPSILON = 1e-06
WIDTH = 128
MESH = pl.DeviceIdType.MESH


def kernel(
    nz, npos, share, dos, ph, wt, out, ex_out, ar_out,
    part, r1, r2, r3, xt, ex, e1, e2, e3, ar, a1, a2, a3, pp, pr, pf,
    s_sem, v_sem, s3_sem, v3_sem, es_sem, ev_sem, es3_sem, ev3_sem, ps_sem, pv_sem,
):
    samples, variants = dos.shape
    traits = ph.shape[1]
    chunks, w, block = part.shape[0], part.shape[4], part.shape[5]
    tile = 2 * block
    me = lax.axis_index("samp")
    mp = lax.axis_index("pos")
    mx = lax.rem(me, 2)
    my = lax.rem(me // 2, 2)
    mz = me // 4
    xp = (mz * 4 + my * 2 + (1 - mx), mp)
    yp = (mz * 4 + (1 - my) * 2 + mx, mp)

    def zpeer(d):
        return lax.rem(mz + d, nz)

    def zdev(d):
        return (zpeer(d) * 4 + my * 2 + mx, mp)

    def ppeer(d):
        return lax.rem(mp + d, npos)

    barrier = pltpu.get_barrier_semaphore()
    peers = [xp, yp] + [zdev(d) for d in range(1, nz)]
    peers += [(me, ppeer(d)) for d in range(1, npos)]
    for peer in peers:
        pl.semaphore_signal(barrier, inc=1, device_id=peer, device_id_type=MESH)
    pl.semaphore_wait(barrier, len(peers))

    def remote(src, dst, send, recv, dev):
        return pltpu.make_async_remote_copy(
            src_ref=src, dst_ref=dst, send_sem=send, recv_sem=recv,
            device_id=dev, device_id_type=MESH,
        )

    def order(c):
        return (mx, my, xp, yp) if c % 2 == 0 else (my, mx, yp, xp)

    def compute(c):
        cols = slice(c * w, (c + 1) * w)
        xt[...] = dos[:, cols].T

        def body(i, carry):
            res = jnp.dot(
                xt[...],
                ph[:, pl.ds(pl.multiple_of(i * tile, tile), tile)],
                preferred_element_type=jnp.float32,
            )
            z, y = i // 2, lax.rem(i, 2)
            for x in range(2):
                val = res[:, x * block : (x + 1) * block]
                if c % 2 == 0:
                    part[c, x, y, z] = val
                else:
                    part[c, y, x, z] = val
            return carry

        lax.fori_loop(0, 2 * nz, body, 0)

    def copy1(c):
        f, _, dev, _ = order(c)
        return remote(part.at[c, 1 - f], r1.at[c], s_sem.at[0, c], v_sem.at[0, c], dev)

    def copy2(c):
        f, s, _, dev = order(c)
        return remote(part.at[c, f, 1 - s], r2.at[c], s_sem.at[1, c], v_sem.at[1, c], dev)

    def copy3(c, d):
        f, s, _, _ = order(c)
        return remote(
            part.at[c, f, s, zpeer(d)], r3.at[c, d - 1],
            s3_sem.at[c, d - 1], v3_sem.at[c, d - 1], zdev(d),
        )

    def add1(c, other):
        f, s, _, _ = order(c)
        k = 1 - s if other else s

        def body(z, carry):
            part[c, f, k, z] = part[c, f, k, z] + r1[c, k, z]
            return carry

        lax.fori_loop(0, nz, body, 0)

    def stage2(c):
        copy1(c).wait_recv()
        add1(c, True)
        copy2(c).start()
        add1(c, False)

    def stage3(c):
        f, s, _, _ = order(c)
        copy2(c).wait_recv()

        def body(z, carry):
            part[c, f, s, z] = part[c, f, s, z] + r2[c, z]
            return carry

        lax.fori_loop(0, nz, body, 0)
        for d in range(nz - 1, 0, -1):
            copy3(c, d).start()

    def finish(c):
        f, s, _, _ = order(c)
        total = part[c, f, s, mz]
        for d in range(1, nz):
            copy3(c, d).wait_recv()
            total = total + r3[c, d - 1]
        out[c] = total

    def pcopy(d):
        return remote(
            pp.at[ppeer(d)], pr.at[d - 1], ps_sem.at[d - 1], pv_sem.at[d - 1],
            (me, ppeer(d)),
        )

    def predict():
        step = min(samples, 256)

        def body(i, carry):
            rows = pl.ds(pl.multiple_of(i * step, step), step)
            res = lax.dot_general(
                wt[...], dos[rows, :], (((1,), (1,)), ((), ())),
                preferred_element_type=jnp.float32,
            )
            for q in range(npos):
                pp[q, :, rows] = res[q * share : (q + 1) * share]
            return carry

        lax.fori_loop(0, samples // step, body, 0)
        for d in range(1, npos):
            pcopy(d).start()

    def squares(ref, cols, width):
        step = min(samples, 128)

        def body(i, acc):
            v = ref[pl.ds(pl.multiple_of(i * step, step), step), cols].astype(jnp.float32)
            return acc + jnp.sum(v * v, axis=0, keepdims=True)

        return lax.fori_loop(0, samples // step, body, jnp.zeros((1, width), jnp.float32))

    def small():
        pred = pp[mp]
        for d in range(1, npos):
            pcopy(d).wait_recv()
            pred = pred + pr[d - 1]
        pf[...] = jnp.zeros_like(pf)
        pf[0:share, :] = pred
        full = pf[...]
        low = full.astype(jnp.bfloat16)
        ar[chunks : chunks + pf.shape[0], :] = jnp.broadcast_to(
            jnp.sum(full * full, axis=1, keepdims=True), (pf.shape[0], w)
        )
        for c in range(chunks):
            ar[c : c + 1, :] = squares(dos, slice(c * w, (c + 1) * w), w)
        g = pf.shape[0]

        def body(i, carry):
            cols = pl.ds(pl.multiple_of(i * tile, tile), tile)
            res = jnp.dot(low, ph[:, cols], preferred_element_type=jnp.float32)
            tsq = jnp.broadcast_to(squares(ph, cols, tile), (8, tile))
            z, y = i // 2, lax.rem(i, 2)
            for x in range(2):
                ex[x, y, z, 0:g, :] = res[:, x * block : (x + 1) * block]
                ex[x, y, z, g : g + 8, :] = tsq[:, x * block : (x + 1) * block]
            return carry

        lax.fori_loop(0, 2 * nz, body, 0)

    ecopy1 = remote(ex.at[1 - mx], e1, es_sem.at[0], ev_sem.at[0], xp)
    acopy1 = remote(ar, a1, es_sem.at[1], ev_sem.at[1], xp)
    ecopy2 = remote(ex.at[mx, 1 - my], e2, es_sem.at[2], ev_sem.at[2], yp)
    acopy2 = remote(ar_out, a2, es_sem.at[3], ev_sem.at[3], yp)

    def ecopy3(d):
        return remote(
            ex.at[mx, my, zpeer(d)], e3.at[d - 1],
            es3_sem.at[0, d - 1], ev3_sem.at[0, d - 1], zdev(d),
        )

    def acopy3(d):
        return remote(
            ar, a3.at[d - 1], es3_sem.at[1, d - 1], ev3_sem.at[1, d - 1], zdev(d)
        )

    def small1():
        ecopy1.start()
        acopy1.start()

    def small2():
        ecopy1.wait_recv()
        ex[mx] = ex[mx] + e1[...]
        ecopy2.start()
        acopy1.wait()
        ar_out[...] = ar[...] + a1[...]
        acopy2.start()

    def small3():
        ecopy2.wait_recv()
        ex[mx, my] = ex[mx, my] + e2[...]
        acopy2.wait()
        ar[...] = ar_out[...] + a2[...]
        for d in range(nz - 1, 0, -1):
            ecopy3(d).start()
            acopy3(d).start()

    def small4():
        total = ex[mx, my, mz]
        sums = ar[...]
        for d in range(1, nz):
            ecopy3(d).wait_recv()
            acopy3(d).wait_recv()
            total = total + e3[d - 1]
            sums = sums + a3[d - 1]
        ex_out[...] = total
        ar_out[...] = sums

    pairs = chunks // 2
    for t in range(pairs + 3):
        if t == 0:
            compute(0)
            copy1(0).start()
            compute(1)
            copy1(1).start()
        if t + 1 < pairs:
            for c in (2 * t + 2, 2 * t + 3):
                compute(c)
                copy1(c).start()
        if t == 0:
            predict()
        if t == 1:
            small()
            small1()
        if t == 2:
            small2()
        if t == 3:
            small3()
        if 0 <= t < pairs:
            for c in (2 * t, 2 * t + 1):
                stage2(c)
        if 0 <= t - 1 < pairs:
            for c in (2 * t - 2, 2 * t - 1):
                stage3(c)
        if 0 <= t - 2 < pairs:
            for c in (2 * t - 4, 2 * t - 3):
                finish(c)
    small4()
    for c in range(chunks):
        copy1(c).wait_send()
        copy2(c).wait_send()
        for d in range(1, nz):
            copy3(c, d).wait_send()
    ecopy1.wait_send()
    ecopy2.wait_send()
    for d in range(1, nz):
        ecopy3(d).wait_send()
        acopy3(d).wait_send()
    for d in range(1, npos):
        pcopy(d).wait_send()


def reduce_all(dosages, phenotypes, masked_t, n, npos, share):
    samples, variants = dosages.shape
    traits = phenotypes.shape[1]
    nz = n // 4
    block = traits // n
    w = WIDTH
    chunks = variants // w
    g = -(-share // 16) * 16
    f32 = jnp.float32
    vm = pltpu.VMEM
    dma = pltpu.SemaphoreType.DMA
    nq = max(npos - 1, 1)
    scratch = [
        vm((chunks, 2, 2, nz, w, block), f32),
        vm((chunks, 2, nz, w, block), f32),
        vm((chunks, nz, w, block), f32),
        vm((chunks, nz - 1, w, block), f32),
        vm((w, samples), jnp.bfloat16),
        vm((2, 2, nz, g + 8, block), f32),
        vm((2, nz, g + 8, block), f32),
        vm((nz, g + 8, block), f32),
        vm((nz - 1, g + 8, block), f32),
        vm((chunks + g, w), f32),
        vm((chunks + g, w), f32),
        vm((chunks + g, w), f32),
        vm((nz - 1, chunks + g, w), f32),
        vm((npos, share, samples), f32),
        vm((nq, share, samples), f32),
        vm((g, samples), f32),
        dma((2, chunks)), dma((2, chunks)),
        dma((chunks, nz - 1)), dma((chunks, nz - 1)),
        dma((4,)), dma((4,)),
        dma((2, nz - 1)), dma((2, nz - 1)),
        dma((nq,)), dma((nq,)),
    ]
    flops = 2 * samples * variants * traits
    return pl.pallas_call(
        functools.partial(kernel, nz, npos, share),
        out_shape=(
            jax.ShapeDtypeStruct((chunks, w, block), f32),
            jax.ShapeDtypeStruct((g + 8, block), f32),
            jax.ShapeDtypeStruct((chunks + g, w), f32),
        ),
        in_specs=[pl.BlockSpec(memory_space=pltpu.VMEM)] * 3,
        out_specs=[pl.BlockSpec(memory_space=pltpu.VMEM)] * 3,
        scratch_shapes=scratch,
        compiler_params=pltpu.CompilerParams(
            collective_id=0, has_side_effects=True, vmem_limit_bytes=60 * 1024 * 1024
        ),
        cost_estimate=pl.CostEstimate(
            flops=flops, bytes_accessed=2 * samples * (variants + traits), transcendentals=0
        ),
    )(dosages, phenotypes, masked_t)


def per_device(dosages, phenotypes, gene_weights, gene_start, gene_end):
    variants = dosages.shape[1]
    genes = gene_weights.shape[1]
    n, npos = lax.axis_size("samp"), lax.axis_size("pos")
    share = genes // npos
    offset = lax.axis_index("pos") * variants
    position = offset + lax.broadcasted_iota(jnp.int32, (genes, variants), 1)
    inside = (position >= gene_start[:, None]) & (position < gene_end[:, None])
    weights_t = gene_weights.T
    masked_t = jnp.where(inside, weights_t, jnp.zeros_like(weights_t))
    out, extra, sums = reduce_all(dosages, phenotypes, masked_t, n, npos, share)
    samples = dosages.shape[0] * n
    chunks = out.shape[0]
    g = sums.shape[0] - chunks
    mean_dose = sums[:chunks].reshape(-1) / samples
    mean_pred = sums[chunks : chunks + share, 0] / samples
    mean_trait = extra[g] / samples
    marginal = out.reshape(variants, -1).T
    variant_z = marginal / jnp.sqrt(
        samples * (mean_trait[:, None] + EPSILON) * (mean_dose[None, :] + EPSILON)
    )
    gene_z = extra[:share].T / jnp.sqrt(
        samples * (mean_trait[:, None] + EPSILON) * (mean_pred[None, :] + EPSILON)
    )
    return (variant_z, gene_z)


def solution(mesh):
    return jax.shard_map(
        per_device,
        mesh=mesh,
        in_specs=(P("samp", "pos"), P("samp", None), P("pos", None), P(), P()),
        out_specs=(P("samp", "pos"), P("samp", "pos")),
        check_vma=False,
    )
```

```python
import functools

import jax
import jax.numpy as jnp
from jax import lax
from jax.experimental import pallas as pl
from jax.experimental.pallas import tpu as pltpu
from jax.sharding import PartitionSpec as P

EPSILON = 1e-06
WIDTH = 128
MESH = pl.DeviceIdType.MESH


def kernel(
    nz, npos, share, dos_hbm, ph_hbm, wt, out, ex_out, ar_out,
    dos, ph, part, r1, r2, r3, zpart, z1, z2, z3, xt, ex, e1, e2, e3, ar, a1, a2, a3, pp, pr, pf,
    s_sem, v_sem, s3_sem, v3_sem, es_sem, ev_sem, es3_sem, ev3_sem, ps_sem, pv_sem,
    dl_sem, pl_sem,
):
    samples, variants = dos.shape
    traits = ph.shape[1]
    chunks, w, block = out.shape
    tile = 2 * block
    me = lax.axis_index("samp")
    mp = lax.axis_index("pos")
    mx = lax.rem(me, 2)
    my = lax.rem(me // 2, 2)
    mz = me // 4
    xp = (mz * 4 + my * 2 + (1 - mx), mp)
    yp = (mz * 4 + (1 - my) * 2 + mx, mp)

    def zpeer(d):
        return lax.rem(mz + d, nz)

    def zdev(d):
        return (zpeer(d) * 4 + my * 2 + mx, mp)

    def ppeer(d):
        return lax.rem(mp + d, npos)

    def load_dos(c):
        cols = slice(c * w, (c + 1) * w)
        return pltpu.make_async_copy(dos_hbm.at[:, cols], dos.at[:, cols], dl_sem.at[c])

    def load_ph(i):
        cols = pl.ds(pl.multiple_of(i * tile, tile), tile)
        return pltpu.make_async_copy(ph_hbm.at[:, cols], ph.at[:, cols], pl_sem.at[i])

    load_dos(2).start()
    for i in range(2 * nz):
        load_ph(i).start()
    for c in range(chunks):
        if c != 2:
            load_dos(c).start()

    barrier = pltpu.get_barrier_semaphore()
    peers = [xp, yp] + [zdev(d) for d in range(1, nz)]
    peers += [(me, ppeer(d)) for d in range(1, npos)]
    for peer in peers:
        pl.semaphore_signal(barrier, inc=1, device_id=peer, device_id_type=MESH)
    pl.semaphore_wait(barrier, len(peers))

    def remote(src, dst, send, recv, dev):
        return pltpu.make_async_remote_copy(
            src_ref=src, dst_ref=dst, send_sem=send, recv_sem=recv,
            device_id=dev, device_id_type=MESH,
        )

    def order(c):
        return (mx, my, xp, yp) if c % 2 == 0 else (my, mx, yp, xp)

    def compute(c, first=False):
        cols = slice(c * w, (c + 1) * w)
        if c < 6:
            load_dos(c).wait()
        xt[...] = dos[:, cols].T

        def body(i, carry):
            if first:
                load_ph(i).wait()
            res = jnp.dot(
                xt[...],
                ph[:, pl.ds(pl.multiple_of(i * tile, tile), tile)],
                preferred_element_type=jnp.float32,
            )
            z, y = i // 2, lax.rem(i, 2)
            for x in range(2):
                val = res[:, x * block : (x + 1) * block]
                a, b = (x, y) if c % 2 == 0 else (y, x)
                if c < 2:
                    zpart[c, z, a, b] = val
                else:
                    part[c - 2, a, b, z] = val
            return carry

        lax.fori_loop(0, 2 * nz, body, 0)

    def copy1(c):
        f, _, dev, _ = order(c)
        return remote(part.at[c - 2, 1 - f], r1.at[c - 2], s_sem.at[0, c], v_sem.at[0, c], dev)

    def copy2(c):
        f, s, _, dev = order(c)
        return remote(part.at[c - 2, f, 1 - s], r2.at[c - 2], s_sem.at[1, c], v_sem.at[1, c], dev)

    def copy3(c, d):
        f, s, _, _ = order(c)
        return remote(
            part.at[c - 2, f, s, zpeer(d)], r3.at[c - 2, d - 1],
            s3_sem.at[c, d - 1], v3_sem.at[c, d - 1], zdev(d),
        )

    def add1(c, other):
        f, s, _, _ = order(c)
        k = 1 - s if other else s

        def body(z, carry):
            part[c - 2, f, k, z] = part[c - 2, f, k, z] + r1[c - 2, k, z]
            return carry

        lax.fori_loop(0, nz, body, 0)

    def stage2(c):
        copy1(c).wait_recv()
        add1(c, True)
        copy2(c).start()
        add1(c, False)

    def stage3(c):
        f, s, _, _ = order(c)
        copy2(c).wait_recv()

        def body(z, carry):
            part[c - 2, f, s, z] = part[c - 2, f, s, z] + r2[c - 2, z]
            return carry

        lax.fori_loop(0, nz, body, 0)
        for d in range(nz - 1, 0, -1):
            copy3(c, d).start()

    def finish(c):
        f, s, _, _ = order(c)
        total = part[c - 2, f, s, mz]
        for d in range(1, nz):
            copy3(c, d).wait_recv()
            total = total + r3[c - 2, d - 1]
        out[c] = total

    def zcopy1(c, d):
        return remote(
            zpart.at[c, zpeer(d)], z1.at[c, d - 1],
            s3_sem.at[c, d - 1], v3_sem.at[c, d - 1], zdev(d),
        )

    def zcopy2(c):
        f, _, dev, _ = order(c)
        return remote(
            zpart.at[c, mz, 1 - f], z2.at[c], s_sem.at[0, c], v_sem.at[0, c], dev
        )

    def zcopy3(c):
        f, s, _, dev = order(c)
        return remote(
            zpart.at[c, mz, f, 1 - s], z3.at[c], s_sem.at[1, c], v_sem.at[1, c], dev
        )

    def zstage2(c):
        f, _, _, _ = order(c)
        for d in range(1, nz):
            zcopy1(c, d).wait_recv()
        for k in range(2):
            for m in range(2):
                total = zpart[c, mz, k, m]
                for d in range(1, nz):
                    total = total + z1[c, d - 1, k, m]
                zpart[c, mz, k, m] = total
        zcopy2(c).start()

    def zstage3(c):
        f, _, _, _ = order(c)
        zcopy2(c).wait_recv()
        for m in range(2):
            zpart[c, mz, f, m] = zpart[c, mz, f, m] + z2[c, m]
        zcopy3(c).start()

    def zfinish(c):
        f, s, _, _ = order(c)
        zcopy3(c).wait_recv()
        out[c] = zpart[c, mz, f, s] + z3[c]

    def pcopy(d):
        return remote(
            pp.at[ppeer(d)], pr.at[d - 1], ps_sem.at[d - 1], pv_sem.at[d - 1],
            (me, ppeer(d)),
        )

    def predict():
        step = min(samples, 256)

        def body(i, carry):
            rows = pl.ds(pl.multiple_of(i * step, step), step)
            res = lax.dot_general(
                wt[...], dos[rows, :], (((1,), (1,)), ((), ())),
                preferred_element_type=jnp.float32,
            )
            for q in range(npos):
                pp[q, :, rows] = res[q * share : (q + 1) * share]
            return carry

        lax.fori_loop(0, samples // step, body, 0)
        for d in range(1, npos):
            pcopy(d).start()

    def squares(ref, cols, width):
        step = min(samples, 128)

        def body(i, acc):
            v = ref[pl.ds(pl.multiple_of(i * step, step), step), cols].astype(jnp.float32)
            return acc + jnp.sum(v * v, axis=0, keepdims=True)

        return lax.fori_loop(0, samples // step, body, jnp.zeros((1, width), jnp.float32))

    def small():
        pred = pp[mp]
        for d in range(1, npos):
            pcopy(d).wait_recv()
            pred = pred + pr[d - 1]
        pf[...] = jnp.zeros_like(pf)
        pf[0:share, :] = pred
        full = pf[...]
        low = full.astype(jnp.bfloat16)
        ar[chunks : chunks + pf.shape[0], :] = jnp.broadcast_to(
            jnp.sum(full * full, axis=1, keepdims=True), (pf.shape[0], w)
        )
        for c in range(chunks):
            ar[c : c + 1, :] = squares(dos, slice(c * w, (c + 1) * w), w)
        g = pf.shape[0]

        def body(i, carry):
            cols = pl.ds(pl.multiple_of(i * tile, tile), tile)
            res = jnp.dot(low, ph[:, cols], preferred_element_type=jnp.float32)
            tsq = jnp.broadcast_to(squares(ph, cols, tile), (8, tile))
            z, y = i // 2, lax.rem(i, 2)
            for x in range(2):
                ex[x, y, z, 0:g, :] = res[:, x * block : (x + 1) * block]
                ex[x, y, z, g : g + 8, :] = tsq[:, x * block : (x + 1) * block]
            return carry

        lax.fori_loop(0, 2 * nz, body, 0)

    ecopy1 = remote(ex.at[1 - mx], e1, es_sem.at[0], ev_sem.at[0], xp)
    acopy1 = remote(ar, a1, es_sem.at[1], ev_sem.at[1], xp)
    ecopy2 = remote(ex.at[mx, 1 - my], e2, es_sem.at[2], ev_sem.at[2], yp)
    acopy2 = remote(ar_out, a2, es_sem.at[3], ev_sem.at[3], yp)

    def ecopy3(d):
        return remote(
            ex.at[mx, my, zpeer(d)], e3.at[d - 1],
            es3_sem.at[0, d - 1], ev3_sem.at[0, d - 1], zdev(d),
        )

    def acopy3(d):
        return remote(
            ar, a3.at[d - 1], es3_sem.at[1, d - 1], ev3_sem.at[1, d - 1], zdev(d)
        )

    def small1():
        ecopy1.start()
        acopy1.start()

    def small2():
        ecopy1.wait_recv()
        ex[mx] = ex[mx] + e1[...]
        ecopy2.start()
        acopy1.wait()
        ar_out[...] = ar[...] + a1[...]
        acopy2.start()

    def small3():
        ecopy2.wait_recv()
        ex[mx, my] = ex[mx, my] + e2[...]
        acopy2.wait()
        ar[...] = ar_out[...] + a2[...]
        for d in range(nz - 1, 0, -1):
            ecopy3(d).start()
            acopy3(d).start()

    def small4():
        total = ex[mx, my, mz]
        sums = ar[...]
        for d in range(1, nz):
            ecopy3(d).wait_recv()
            acopy3(d).wait_recv()
            total = total + e3[d - 1]
            sums = sums + a3[d - 1]
        ex_out[...] = total
        ar_out[...] = sums

    pairs = chunks // 2 - 1
    for t in range(max(pairs + 5, 9)):
        if t == 0:
            compute(2, first=True)
            copy1(2).start()
            compute(3)
            copy1(3).start()
            for c in range(2):
                compute(c)
                for d in range(nz - 1, 0, -1):
                    zcopy1(c, d).start()
        if t + 1 < pairs:
            for c in (2 * t + 4, 2 * t + 5):
                compute(c)
                copy1(c).start()
        if 0 <= t < pairs:
            for c in (2 * t + 2, 2 * t + 3):
                stage2(c)
        if t == 0:
            for c in range(chunks):
                if c >= min(6, 2 * pairs + 2):
                    load_dos(c).wait()
            predict()
        if t == 1:
            small()
            small1()
        if t == 2:
            small2()
        if t == 3:
            small3()
        if 0 <= t - 1 < pairs:
            for c in (2 * t, 2 * t + 1):
                stage3(c)
        if t == 4:
            zstage2(0)
            zstage2(1)
        if t == 5:
            zstage3(0)
            zstage3(1)
        if t == 6:
            small4()
            zfinish(0)
            zfinish(1)
        if 0 <= t - 4 < pairs:
            for c in (2 * t - 6, 2 * t - 5):
                finish(c)
    for c in range(2):
        zcopy2(c).wait_send()
        zcopy3(c).wait_send()
        for d in range(1, nz):
            zcopy1(c, d).wait_send()
    for c in range(2, chunks):
        copy1(c).wait_send()
        copy2(c).wait_send()
        for d in range(1, nz):
            copy3(c, d).wait_send()
    ecopy1.wait_send()
    ecopy2.wait_send()
    for d in range(1, nz):
        ecopy3(d).wait_send()
        acopy3(d).wait_send()
    for d in range(1, npos):
        pcopy(d).wait_send()


def reduce_all(dosages, phenotypes, masked_t, n, npos, share):
    samples, variants = dosages.shape
    traits = phenotypes.shape[1]
    nz = n // 4
    block = traits // n
    w = WIDTH
    chunks = variants // w
    g = -(-share // 16) * 16
    f32 = jnp.float32
    vm = pltpu.VMEM
    dma = pltpu.SemaphoreType.DMA
    nq = max(npos - 1, 1)
    scratch = [
        vm((samples, variants), jnp.bfloat16),
        vm((samples, traits), jnp.bfloat16),
        vm((chunks - 2, 2, 2, nz, w, block), f32),
        vm((chunks - 2, 2, nz, w, block), f32),
        vm((chunks - 2, nz, w, block), f32),
        vm((chunks - 2, nz - 1, w, block), f32),
        vm((2, nz, 2, 2, w, block), f32),
        vm((2, nz - 1, 2, 2, w, block), f32),
        vm((2, 2, w, block), f32),
        vm((2, w, block), f32),
        vm((w, samples), jnp.bfloat16),
        vm((2, 2, nz, g + 8, block), f32),
        vm((2, nz, g + 8, block), f32),
        vm((nz, g + 8, block), f32),
        vm((nz - 1, g + 8, block), f32),
        vm((chunks + g, w), f32),
        vm((chunks + g, w), f32),
        vm((chunks + g, w), f32),
        vm((nz - 1, chunks + g, w), f32),
        vm((npos, share, samples), f32),
        vm((nq, share, samples), f32),
        vm((g, samples), f32),
        dma((2, chunks)), dma((2, chunks)),
        dma((chunks, nz - 1)), dma((chunks, nz - 1)),
        dma((4,)), dma((4,)),
        dma((2, nz - 1)), dma((2, nz - 1)),
        dma((nq,)), dma((nq,)),
        dma((chunks,)), dma((2 * nz,)),
    ]
    flops = 2 * samples * variants * traits
    return pl.pallas_call(
        functools.partial(kernel, nz, npos, share),
        out_shape=(
            jax.ShapeDtypeStruct((chunks, w, block), f32),
            jax.ShapeDtypeStruct((g + 8, block), f32),
            jax.ShapeDtypeStruct((chunks + g, w), f32),
        ),
        in_specs=[pl.BlockSpec(memory_space=pl.ANY)] * 2
        + [pl.BlockSpec(memory_space=pltpu.VMEM)],
        out_specs=[pl.BlockSpec(memory_space=pltpu.VMEM)] * 3,
        scratch_shapes=scratch,
        compiler_params=pltpu.CompilerParams(
            collective_id=0, has_side_effects=True, vmem_limit_bytes=60 * 1024 * 1024
        ),
        cost_estimate=pl.CostEstimate(
            flops=flops, bytes_accessed=2 * samples * (variants + traits), transcendentals=0
        ),
    )(dosages, phenotypes, masked_t)


def per_device(dosages, phenotypes, gene_weights, gene_start, gene_end):
    variants = dosages.shape[1]
    genes = gene_weights.shape[1]
    n, npos = lax.axis_size("samp"), lax.axis_size("pos")
    share = genes // npos
    offset = lax.axis_index("pos") * variants
    position = offset + lax.broadcasted_iota(jnp.int32, (genes, variants), 1)
    inside = (position >= gene_start[:, None]) & (position < gene_end[:, None])
    weights_t = gene_weights.T
    masked_t = jnp.where(inside, weights_t, jnp.zeros_like(weights_t))
    out, extra, sums = reduce_all(dosages, phenotypes, masked_t, n, npos, share)
    samples = dosages.shape[0] * n
    chunks = out.shape[0]
    g = sums.shape[0] - chunks
    mean_dose = sums[:chunks].reshape(-1) / samples
    mean_pred = sums[chunks : chunks + share, 0] / samples
    mean_trait = extra[g] / samples
    marginal = out.reshape(variants, -1).T
    variant_z = marginal / jnp.sqrt(
        samples * (mean_trait[:, None] + EPSILON) * (mean_dose[None, :] + EPSILON)
    )
    gene_z = extra[:share].T / jnp.sqrt(
        samples * (mean_trait[:, None] + EPSILON) * (mean_pred[None, :] + EPSILON)
    )
    return (variant_z, gene_z)


def solution(mesh):
    return jax.shard_map(
        per_device,
        mesh=mesh,
        in_specs=(P("samp", "pos"), P("samp", None), P("pos", None), P(), P()),
        out_specs=(P("samp", "pos"), P("samp", "pos")),
        check_vma=False,
    )
```

```python
import functools

import jax
import jax.numpy as jnp
from jax import lax
from jax.experimental import pallas as pl
from jax.experimental.pallas import tpu as pltpu
from jax.sharding import PartitionSpec as P

EPSILON = 1e-06
WIDTH = 128
MESH = pl.DeviceIdType.MESH


def kernel(
    nz, npos, share, dos_hbm, ph_hbm, wt, out, ex_out, ar_out,
    dos, ph, part, r1, r2, r3, zpart, z1, z2, z3, xt, ex, e1, e2, e3, ar, a1, a2, a3, pp, pr, pf,
    s_sem, v_sem, s3_sem, v3_sem, es_sem, ev_sem, es3_sem, ev3_sem, ps_sem, pv_sem,
    dl_sem, pl_sem,
):
    samples, variants = dos.shape
    traits = ph.shape[1]
    chunks, w, block = out.shape
    tile = 2 * block
    me = lax.axis_index("samp")
    mp = lax.axis_index("pos")
    mx = lax.rem(me, 2)
    my = lax.rem(me // 2, 2)
    mz = me // 4
    xp = (mz * 4 + my * 2 + (1 - mx), mp)
    yp = (mz * 4 + (1 - my) * 2 + mx, mp)

    def zpeer(d):
        return lax.rem(mz + d, nz)

    def zdev(d):
        return (zpeer(d) * 4 + my * 2 + mx, mp)

    def ppeer(d):
        return lax.rem(mp + d, npos)

    def load_dos(c):
        cols = slice(c * w, (c + 1) * w)
        return pltpu.make_async_copy(dos_hbm.at[:, cols], dos.at[:, cols], dl_sem.at[c])

    def load_ph(i):
        cols = pl.ds(pl.multiple_of(i * tile, tile), tile)
        return pltpu.make_async_copy(ph_hbm.at[:, cols], ph.at[:, cols], pl_sem.at[i])

    load_dos(2).start()
    for i in range(2 * nz):
        load_ph(i).start()
    for c in range(chunks):
        if c != 2:
            load_dos(c).start()

    barrier = pltpu.get_barrier_semaphore()
    peers = [xp, yp] + [zdev(d) for d in range(1, nz)]
    peers += [(me, ppeer(d)) for d in range(1, npos)]
    for peer in peers:
        pl.semaphore_signal(barrier, inc=1, device_id=peer, device_id_type=MESH)
    pl.semaphore_wait(barrier, len(peers))

    def remote(src, dst, send, recv, dev):
        return pltpu.make_async_remote_copy(
            src_ref=src, dst_ref=dst, send_sem=send, recv_sem=recv,
            device_id=dev, device_id_type=MESH,
        )

    def order(c):
        return (mx, my, xp, yp) if c % 2 == 0 else (my, mx, yp, xp)

    def compute(c, first=False):
        cols = slice(c * w, (c + 1) * w)
        if c < 8:
            load_dos(c).wait()
        xt[...] = dos[:, cols].T

        def body(i, carry):
            if first:
                load_ph(i).wait()
            res = jnp.dot(
                xt[...],
                ph[:, pl.ds(pl.multiple_of(i * tile, tile), tile)],
                preferred_element_type=jnp.float32,
            )
            z, y = i // 2, lax.rem(i, 2)
            for x in range(2):
                val = res[:, x * block : (x + 1) * block]
                a, b = (x, y) if c % 2 == 0 else (y, x)
                if c < 2:
                    zpart[c, z, a, b] = val
                else:
                    part[c - 2, a, b, z] = val
            return carry

        lax.fori_loop(0, 2 * nz, body, 0)

    def copy1(c):
        f, _, dev, _ = order(c)
        return remote(part.at[c - 2, 1 - f], r1.at[c - 2], s_sem.at[0, c], v_sem.at[0, c], dev)

    def copy2(c):
        f, s, _, dev = order(c)
        return remote(part.at[c - 2, f, 1 - s], r2.at[c - 2], s_sem.at[1, c], v_sem.at[1, c], dev)

    def copy3(c, d):
        f, s, _, _ = order(c)
        return remote(
            part.at[c - 2, f, s, zpeer(d)], r3.at[c - 2, d - 1],
            s3_sem.at[c, d - 1], v3_sem.at[c, d - 1], zdev(d),
        )

    def add1(c, other):
        f, s, _, _ = order(c)
        k = 1 - s if other else s

        def body(z, carry):
            part[c - 2, f, k, z] = part[c - 2, f, k, z] + r1[c - 2, k, z]
            return carry

        lax.fori_loop(0, nz, body, 0)

    def stage2(c):
        copy1(c).wait_recv()
        add1(c, True)
        copy2(c).start()
        add1(c, False)

    def stage3(c):
        f, s, _, _ = order(c)
        copy2(c).wait_recv()

        def body(z, carry):
            part[c - 2, f, s, z] = part[c - 2, f, s, z] + r2[c - 2, z]
            return carry

        lax.fori_loop(0, nz, body, 0)
        for d in range(nz - 1, 0, -1):
            copy3(c, d).start()

    def finish(c):
        f, s, _, _ = order(c)
        total = part[c - 2, f, s, mz]
        for d in range(1, nz):
            copy3(c, d).wait_recv()
            total = total + r3[c - 2, d - 1]
        out[c] = total

    def zcopy1(c, d):
        return remote(
            zpart.at[c, zpeer(d)], z1.at[c, d - 1],
            s3_sem.at[c, d - 1], v3_sem.at[c, d - 1], zdev(d),
        )

    def zcopy2(c):
        f, _, dev, _ = order(c)
        return remote(
            zpart.at[c, mz, 1 - f], z2.at[c], s_sem.at[0, c], v_sem.at[0, c], dev
        )

    def zcopy3(c):
        f, s, _, dev = order(c)
        return remote(
            zpart.at[c, mz, f, 1 - s], z3.at[c], s_sem.at[1, c], v_sem.at[1, c], dev
        )

    def zstage2(c):
        f, _, _, _ = order(c)
        for d in range(1, nz):
            zcopy1(c, d).wait_recv()
        for k in range(2):
            for m in range(2):
                total = zpart[c, mz, k, m]
                for d in range(1, nz):
                    total = total + z1[c, d - 1, k, m]
                zpart[c, mz, k, m] = total
        zcopy2(c).start()

    def zstage3(c):
        f, _, _, _ = order(c)
        zcopy2(c).wait_recv()
        for m in range(2):
            zpart[c, mz, f, m] = zpart[c, mz, f, m] + z2[c, m]
        zcopy3(c).start()

    def zfinish(c):
        f, s, _, _ = order(c)
        zcopy3(c).wait_recv()
        out[c] = zpart[c, mz, f, s] + z3[c]

    def pcopy(d):
        return remote(
            pp.at[ppeer(d)], pr.at[d - 1], ps_sem.at[d - 1], pv_sem.at[d - 1],
            (me, ppeer(d)),
        )

    def predict():
        step = min(samples, 256)

        def body(i, carry):
            rows = pl.ds(pl.multiple_of(i * step, step), step)
            res = lax.dot_general(
                wt[...], dos[rows, :], (((1,), (1,)), ((), ())),
                preferred_element_type=jnp.float32,
            )
            for q in range(npos):
                pp[q, :, rows] = res[q * share : (q + 1) * share]
            return carry

        lax.fori_loop(0, samples // step, body, 0)
        for d in range(1, npos):
            pcopy(d).start()

    def squares(ref, cols, width):
        step = min(samples, 256)

        def body(i, acc):
            v = ref[pl.ds(pl.multiple_of(i * step, step), step), cols].astype(jnp.float32)
            return acc + jnp.sum(v * v, axis=0, keepdims=True)

        return lax.fori_loop(0, samples // step, body, jnp.zeros((1, width), jnp.float32))

    def dose_squares():
        for c in range(chunks):
            ar[c : c + 1, :] = squares(dos, slice(c * w, (c + 1) * w), w)

    def small():
        pred = pp[mp]
        for d in range(1, npos):
            pcopy(d).wait_recv()
            pred = pred + pr[d - 1]
        pf[...] = jnp.zeros_like(pf)
        pf[0:share, :] = pred
        full = pf[...]
        low = full.astype(jnp.bfloat16)
        ar[chunks : chunks + pf.shape[0], :] = jnp.broadcast_to(
            jnp.sum(full * full, axis=1, keepdims=True), (pf.shape[0], w)
        )
        g = pf.shape[0]

        def body(i, carry):
            cols = pl.ds(pl.multiple_of(i * tile, tile), tile)
            res = jnp.dot(low, ph[:, cols], preferred_element_type=jnp.float32)
            tsq = jnp.broadcast_to(squares(ph, cols, tile), (8, tile))
            z, y = i // 2, lax.rem(i, 2)
            for x in range(2):
                ex[x, y, z, 0:g, :] = res[:, x * block : (x + 1) * block]
                ex[x, y, z, g : g + 8, :] = tsq[:, x * block : (x + 1) * block]
            return carry

        lax.fori_loop(0, 2 * nz, body, 0)

    ecopy1 = remote(ex.at[1 - mx], e1, es_sem.at[0], ev_sem.at[0], xp)
    acopy1 = remote(ar, a1, es_sem.at[1], ev_sem.at[1], xp)
    ecopy2 = remote(ex.at[mx, 1 - my], e2, es_sem.at[2], ev_sem.at[2], yp)
    acopy2 = remote(ar_out, a2, es_sem.at[3], ev_sem.at[3], yp)

    def ecopy3(d):
        return remote(
            ex.at[mx, my, zpeer(d)], e3.at[d - 1],
            es3_sem.at[0, d - 1], ev3_sem.at[0, d - 1], zdev(d),
        )

    def acopy3(d):
        return remote(
            ar, a3.at[d - 1], es3_sem.at[1, d - 1], ev3_sem.at[1, d - 1], zdev(d)
        )

    def small1():
        ecopy1.start()
        acopy1.start()

    def small2():
        ecopy1.wait_recv()
        ex[mx] = ex[mx] + e1[...]
        ecopy2.start()
        acopy1.wait()
        ar_out[...] = ar[...] + a1[...]
        acopy2.start()

    def small3():
        ecopy2.wait_recv()
        ex[mx, my] = ex[mx, my] + e2[...]
        acopy2.wait()
        ar[...] = ar_out[...] + a2[...]
        for d in range(nz - 1, 0, -1):
            ecopy3(d).start()
            acopy3(d).start()

    def small4():
        total = ex[mx, my, mz]
        sums = ar[...]
        for d in range(1, nz):
            ecopy3(d).wait_recv()
            acopy3(d).wait_recv()
            total = total + e3[d - 1]
            sums = sums + a3[d - 1]
        ex_out[...] = total
        ar_out[...] = sums

    pairs = chunks // 2 - 1
    for t in range(max(pairs + 5, 9)):
        if t == 0:
            compute(2, first=True)
            copy1(2).start()
            compute(3)
            copy1(3).start()
            for c in range(2):
                compute(c)
                for d in range(nz - 1, 0, -1):
                    zcopy1(c, d).start()
            if pairs > 1:
                for c in (4, 5):
                    compute(c)
                    copy1(c).start()
        if t + 2 < pairs:
            for c in (2 * t + 6, 2 * t + 7):
                compute(c)
                copy1(c).start()
        if 0 <= t < pairs:
            for c in (2 * t + 2, 2 * t + 3):
                stage2(c)
        if t == 0:
            for c in range(chunks):
                if c >= min(8, 2 * pairs + 2):
                    load_dos(c).wait()
            predict()
        if t == 1:
            dose_squares()
        if t == 2:
            small()
            small1()
        if t == 3:
            small2()
        if t == 4:
            small3()
        if 0 <= t - 1 < pairs:
            for c in (2 * t, 2 * t + 1):
                stage3(c)
        if t == 4:
            zstage2(0)
            zstage2(1)
        if t == 5:
            zstage3(0)
            zstage3(1)
        if t == 6:
            small4()
            zfinish(0)
            zfinish(1)
        if 0 <= t - 4 < pairs:
            for c in (2 * t - 6, 2 * t - 5):
                finish(c)
    for c in range(2):
        zcopy2(c).wait_send()
        zcopy3(c).wait_send()
        for d in range(1, nz):
            zcopy1(c, d).wait_send()
    for c in range(2, chunks):
        copy1(c).wait_send()
        copy2(c).wait_send()
        for d in range(1, nz):
            copy3(c, d).wait_send()
    ecopy1.wait_send()
    ecopy2.wait_send()
    for d in range(1, nz):
        ecopy3(d).wait_send()
        acopy3(d).wait_send()
    for d in range(1, npos):
        pcopy(d).wait_send()


def reduce_all(dosages, phenotypes, masked_t, n, npos, share):
    samples, variants = dosages.shape
    traits = phenotypes.shape[1]
    nz = n // 4
    block = traits // n
    w = WIDTH
    chunks = variants // w
    g = -(-share // 16) * 16
    f32 = jnp.float32
    vm = pltpu.VMEM
    dma = pltpu.SemaphoreType.DMA
    nq = max(npos - 1, 1)
    scratch = [
        vm((samples, variants), jnp.bfloat16),
        vm((samples, traits), jnp.bfloat16),
        vm((chunks - 2, 2, 2, nz, w, block), f32),
        vm((chunks - 2, 2, nz, w, block), f32),
        vm((chunks - 2, nz, w, block), f32),
        vm((chunks - 2, nz - 1, w, block), f32),
        vm((2, nz, 2, 2, w, block), f32),
        vm((2, nz - 1, 2, 2, w, block), f32),
        vm((2, 2, w, block), f32),
        vm((2, w, block), f32),
        vm((w, samples), jnp.bfloat16),
        vm((2, 2, nz, g + 8, block), f32),
        vm((2, nz, g + 8, block), f32),
        vm((nz, g + 8, block), f32),
        vm((nz - 1, g + 8, block), f32),
        vm((chunks + g, w), f32),
        vm((chunks + g, w), f32),
        vm((chunks + g, w), f32),
        vm((nz - 1, chunks + g, w), f32),
        vm((npos, share, samples), f32),
        vm((nq, share, samples), f32),
        vm((g, samples), f32),
        dma((2, chunks)), dma((2, chunks)),
        dma((chunks, nz - 1)), dma((chunks, nz - 1)),
        dma((4,)), dma((4,)),
        dma((2, nz - 1)), dma((2, nz - 1)),
        dma((nq,)), dma((nq,)),
        dma((chunks,)), dma((2 * nz,)),
    ]
    flops = 2 * samples * variants * traits
    return pl.pallas_call(
        functools.partial(kernel, nz, npos, share),
        out_shape=(
            jax.ShapeDtypeStruct((chunks, w, block), f32),
            jax.ShapeDtypeStruct((g + 8, block), f32),
            jax.ShapeDtypeStruct((chunks + g, w), f32),
        ),
        in_specs=[pl.BlockSpec(memory_space=pl.ANY)] * 2
        + [pl.BlockSpec(memory_space=pltpu.VMEM)],
        out_specs=[pl.BlockSpec(memory_space=pltpu.VMEM)] * 3,
        scratch_shapes=scratch,
        compiler_params=pltpu.CompilerParams(
            collective_id=0, has_side_effects=True, vmem_limit_bytes=60 * 1024 * 1024
        ),
        cost_estimate=pl.CostEstimate(
            flops=flops, bytes_accessed=2 * samples * (variants + traits), transcendentals=0
        ),
    )(dosages, phenotypes, masked_t)


def per_device(dosages, phenotypes, gene_weights, gene_start, gene_end):
    variants = dosages.shape[1]
    genes = gene_weights.shape[1]
    n, npos = lax.axis_size("samp"), lax.axis_size("pos")
    share = genes // npos
    offset = lax.axis_index("pos") * variants
    position = offset + lax.broadcasted_iota(jnp.int32, (genes, variants), 1)
    inside = (position >= gene_start[:, None]) & (position < gene_end[:, None])
    weights_t = gene_weights.T
    masked_t = jnp.where(inside, weights_t, jnp.zeros_like(weights_t))
    out, extra, sums = reduce_all(dosages, phenotypes, masked_t, n, npos, share)
    samples = dosages.shape[0] * n
    chunks = out.shape[0]
    g = sums.shape[0] - chunks
    mean_dose = sums[:chunks].reshape(-1) / samples
    mean_pred = sums[chunks : chunks + share, 0] / samples
    mean_trait = extra[g] / samples
    marginal = out.reshape(variants, -1).T
    variant_z = marginal / jnp.sqrt(
        samples * (mean_trait[:, None] + EPSILON) * (mean_dose[None, :] + EPSILON)
    )
    gene_z = extra[:share].T / jnp.sqrt(
        samples * (mean_trait[:, None] + EPSILON) * (mean_pred[None, :] + EPSILON)
    )
    return (variant_z, gene_z)


def solution(mesh):
    return jax.shard_map(
        per_device,
        mesh=mesh,
        in_specs=(P("samp", "pos"), P("samp", None), P("pos", None), P(), P()),
        out_specs=(P("samp", "pos"), P("samp", "pos")),
        check_vma=False,
    )
```

```python
import functools

import jax
import jax.numpy as jnp
from jax import lax
from jax.experimental import pallas as pl
from jax.experimental.pallas import tpu as pltpu
from jax.sharding import PartitionSpec as P

EPSILON = 1e-06
WIDTH = 128
MESH = pl.DeviceIdType.MESH


def kernel(
    nz, npos, share, dos_hbm, ph_hbm, wt, out, ex_out, ar_out,
    dos, ph, part, r1, r2, r3, zpart, z1, z2, z3, xt, ex, e1, e2, e3, ar, a1, a2, a3, pp, pr, pf,
    s_sem, v_sem, s3_sem, v3_sem, es_sem, ev_sem, es3_sem, ev3_sem, ps_sem, pv_sem,
    dl_sem, pl_sem,
):
    samples, variants = dos.shape
    traits = ph.shape[1]
    chunks, w, block = out.shape
    tile = 2 * block
    me = lax.axis_index("samp")
    mp = lax.axis_index("pos")
    mx = lax.rem(me, 2)
    my = lax.rem(me // 2, 2)
    mz = me // 4
    xp = (mz * 4 + my * 2 + (1 - mx), mp)
    yp = (mz * 4 + (1 - my) * 2 + mx, mp)

    def zpeer(d):
        return lax.rem(mz + d, nz)

    def zdev(d):
        return (zpeer(d) * 4 + my * 2 + mx, mp)

    def ppeer(d):
        return lax.rem(mp + d, npos)

    def load_dos(c):
        cols = slice(c * w, (c + 1) * w)
        return pltpu.make_async_copy(dos_hbm.at[:, cols], dos.at[:, cols], dl_sem.at[c])

    def load_ph(i):
        cols = pl.ds(pl.multiple_of(i * tile, tile), tile)
        return pltpu.make_async_copy(ph_hbm.at[:, cols], ph.at[:, cols], pl_sem.at[i])

    load_dos(2).start()
    for i in range(2 * nz):
        load_ph(i).start()
    for c in range(chunks):
        if c != 2:
            load_dos(c).start()

    barrier = pltpu.get_barrier_semaphore()
    peers = [xp, yp] + [zdev(d) for d in range(1, nz)]
    peers += [(me, ppeer(d)) for d in range(1, npos)]
    for peer in peers:
        pl.semaphore_signal(barrier, inc=1, device_id=peer, device_id_type=MESH)
    pl.semaphore_wait(barrier, len(peers))

    def remote(src, dst, send, recv, dev):
        return pltpu.make_async_remote_copy(
            src_ref=src, dst_ref=dst, send_sem=send, recv_sem=recv,
            device_id=dev, device_id_type=MESH,
        )

    def order(c):
        return (mx, my, xp, yp) if c % 2 == 0 else (my, mx, yp, xp)

    def compute(c, first=False):
        cols = slice(c * w, (c + 1) * w)
        if c < 6:
            load_dos(c).wait()
        xt[...] = dos[:, cols].T

        def body(i, carry):
            if first:
                load_ph(i).wait()
            res = jnp.dot(
                xt[...],
                ph[:, pl.ds(pl.multiple_of(i * tile, tile), tile)],
                preferred_element_type=jnp.float32,
            )
            z, y = i // 2, lax.rem(i, 2)
            for x in range(2):
                val = res[:, x * block : (x + 1) * block]
                a, b = (x, y) if c % 2 == 0 else (y, x)
                if c < 2:
                    zpart[c, z, a, b] = val
                else:
                    part[c - 2, a, b, z] = val
            return carry

        lax.fori_loop(0, 2 * nz, body, 0)

    def copy1(c):
        f, _, dev, _ = order(c)
        return remote(part.at[c - 2, 1 - f], r1.at[c - 2], s_sem.at[0, c], v_sem.at[0, c], dev)

    def copy2(c):
        f, s, _, dev = order(c)
        return remote(part.at[c - 2, f, 1 - s], r2.at[c - 2], s_sem.at[1, c], v_sem.at[1, c], dev)

    def copy3(c, d):
        f, s, _, _ = order(c)
        return remote(
            part.at[c - 2, f, s, zpeer(d)], r3.at[c - 2, d - 1],
            s3_sem.at[c, d - 1], v3_sem.at[c, d - 1], zdev(d),
        )

    def add1(c, other):
        f, s, _, _ = order(c)
        k = 1 - s if other else s

        def body(z, carry):
            part[c - 2, f, k, z] = part[c - 2, f, k, z] + r1[c - 2, k, z]
            return carry

        lax.fori_loop(0, nz, body, 0)

    def stage2(c):
        copy1(c).wait_recv()
        add1(c, True)
        copy2(c).start()
        add1(c, False)

    def stage3(c):
        f, s, _, _ = order(c)
        copy2(c).wait_recv()

        def body(z, carry):
            part[c - 2, f, s, z] = part[c - 2, f, s, z] + r2[c - 2, z]
            return carry

        lax.fori_loop(0, nz, body, 0)
        for d in range(nz - 1, 0, -1):
            copy3(c, d).start()

    def finish(c):
        f, s, _, _ = order(c)
        total = part[c - 2, f, s, mz]
        for d in range(1, nz):
            copy3(c, d).wait_recv()
            total = total + r3[c - 2, d - 1]
        out[c] = total

    def zcopy1(c, d):
        return remote(
            zpart.at[c, zpeer(d)], z1.at[c, d - 1],
            s3_sem.at[c, d - 1], v3_sem.at[c, d - 1], zdev(d),
        )

    def zcopy2(c):
        f, _, dev, _ = order(c)
        return remote(
            zpart.at[c, mz, 1 - f], z2.at[c], s_sem.at[0, c], v_sem.at[0, c], dev
        )

    def zcopy3(c):
        f, s, _, dev = order(c)
        return remote(
            zpart.at[c, mz, f, 1 - s], z3.at[c], s_sem.at[1, c], v_sem.at[1, c], dev
        )

    def zstage2(c):
        f, _, _, _ = order(c)
        for d in range(1, nz):
            zcopy1(c, d).wait_recv()
        for k in range(2):
            for m in range(2):
                total = zpart[c, mz, k, m]
                for d in range(1, nz):
                    total = total + z1[c, d - 1, k, m]
                zpart[c, mz, k, m] = total
        zcopy2(c).start()

    def zstage3(c):
        f, _, _, _ = order(c)
        zcopy2(c).wait_recv()
        for m in range(2):
            zpart[c, mz, f, m] = zpart[c, mz, f, m] + z2[c, m]
        zcopy3(c).start()

    def zfinish(c):
        f, s, _, _ = order(c)
        zcopy3(c).wait_recv()
        out[c] = zpart[c, mz, f, s] + z3[c]

    def pcopy(d):
        return remote(
            pp.at[ppeer(d)], pr.at[d - 1], ps_sem.at[d - 1], pv_sem.at[d - 1],
            (me, ppeer(d)),
        )

    def predict():
        step = min(samples, 256)

        def body(i, carry):
            rows = pl.ds(pl.multiple_of(i * step, step), step)
            res = lax.dot_general(
                wt[...], dos[rows, :], (((1,), (1,)), ((), ())),
                preferred_element_type=jnp.float32,
            )
            for q in range(npos):
                pp[q, :, rows] = res[q * share : (q + 1) * share]
            return carry

        lax.fori_loop(0, samples // step, body, 0)
        for d in range(1, npos):
            pcopy(d).start()

    def squares(ref, cols, width):
        step = min(samples, 256)

        def body(i, acc):
            v = ref[pl.ds(pl.multiple_of(i * step, step), step), cols].astype(jnp.float32)
            return acc + jnp.sum(v * v, axis=0, keepdims=True)

        return lax.fori_loop(0, samples // step, body, jnp.zeros((1, width), jnp.float32))

    def dose_squares():
        for c in range(chunks):
            ar[c : c + 1, :] = squares(dos, slice(c * w, (c + 1) * w), w)

    def small():
        pred = pp[mp]
        for d in range(1, npos):
            pcopy(d).wait_recv()
            pred = pred + pr[d - 1]
        pf[...] = jnp.zeros_like(pf)
        pf[0:share, :] = pred
        full = pf[...]
        low = full.astype(jnp.bfloat16)
        ar[chunks : chunks + pf.shape[0], :] = jnp.broadcast_to(
            jnp.sum(full * full, axis=1, keepdims=True), (pf.shape[0], w)
        )
        g = pf.shape[0]

        def body(i, carry):
            cols = pl.ds(pl.multiple_of(i * tile, tile), tile)
            res = jnp.dot(low, ph[:, cols], preferred_element_type=jnp.float32)
            tsq = jnp.broadcast_to(squares(ph, cols, tile), (8, tile))
            z, y = i // 2, lax.rem(i, 2)
            for x in range(2):
                ex[x, y, z, 0:g, :] = res[:, x * block : (x + 1) * block]
                ex[x, y, z, g : g + 8, :] = tsq[:, x * block : (x + 1) * block]
            return carry

        lax.fori_loop(0, 2 * nz, body, 0)

    ecopy1 = remote(ex.at[1 - mx], e1, es_sem.at[0], ev_sem.at[0], xp)
    acopy1 = remote(ar, a1, es_sem.at[1], ev_sem.at[1], xp)
    ecopy2 = remote(ex.at[mx, 1 - my], e2, es_sem.at[2], ev_sem.at[2], yp)
    acopy2 = remote(ar_out, a2, es_sem.at[3], ev_sem.at[3], yp)

    def ecopy3(d):
        return remote(
            ex.at[mx, my, zpeer(d)], e3.at[d - 1],
            es3_sem.at[0, d - 1], ev3_sem.at[0, d - 1], zdev(d),
        )

    def acopy3(d):
        return remote(
            ar, a3.at[d - 1], es3_sem.at[1, d - 1], ev3_sem.at[1, d - 1], zdev(d)
        )

    def small1():
        ecopy1.start()
        acopy1.start()

    def small2():
        ecopy1.wait_recv()
        ex[mx] = ex[mx] + e1[...]
        ecopy2.start()
        acopy1.wait()
        ar_out[...] = ar[...] + a1[...]
        acopy2.start()

    def small3():
        ecopy2.wait_recv()
        ex[mx, my] = ex[mx, my] + e2[...]
        acopy2.wait()
        ar[...] = ar_out[...] + a2[...]
        for d in range(nz - 1, 0, -1):
            ecopy3(d).start()
            acopy3(d).start()

    def small4():
        total = ex[mx, my, mz]
        sums = ar[...]
        for d in range(1, nz):
            ecopy3(d).wait_recv()
            acopy3(d).wait_recv()
            total = total + e3[d - 1]
            sums = sums + a3[d - 1]
        ex_out[...] = total
        ar_out[...] = sums

    pairs = chunks // 2 - 1
    for t in range(max(pairs + 5, 9)):
        if t == 0:
            compute(2, first=True)
            copy1(2).start()
            compute(3)
            copy1(3).start()
            for c in range(2):
                compute(c)
                for d in range(nz - 1, 0, -1):
                    zcopy1(c, d).start()
        if t + 1 < pairs:
            for c in (2 * t + 4, 2 * t + 5):
                compute(c)
                copy1(c).start()
        if 0 <= t < pairs:
            for c in (2 * t + 2, 2 * t + 3):
                stage2(c)
        if t == 0:
            for c in range(chunks):
                if c >= min(6, 2 * pairs + 2):
                    load_dos(c).wait()
            predict()
        if t == 1:
            dose_squares()
        if t == 2:
            small()
            small1()
        if t == 3:
            small2()
        if t == 4:
            small3()
        if 0 <= t - 1 < pairs:
            for c in (2 * t, 2 * t + 1):
                stage3(c)
        if t == pairs:
            zstage2(0)
            zstage2(1)
        if t == pairs + 1:
            zstage3(0)
            zstage3(1)
        if t == 6:
            small4()
        if t == pairs + 2:
            zfinish(0)
            zfinish(1)
        if 0 <= t - 4 < pairs:
            for c in (2 * t - 6, 2 * t - 5):
                finish(c)
    for c in range(2):
        zcopy2(c).wait_send()
        zcopy3(c).wait_send()
        for d in range(1, nz):
            zcopy1(c, d).wait_send()
    for c in range(2, chunks):
        copy1(c).wait_send()
        copy2(c).wait_send()
        for d in range(1, nz):
            copy3(c, d).wait_send()
    ecopy1.wait_send()
    ecopy2.wait_send()
    for d in range(1, nz):
        ecopy3(d).wait_send()
        acopy3(d).wait_send()
    for d in range(1, npos):
        pcopy(d).wait_send()


def reduce_all(dosages, phenotypes, masked_t, n, npos, share):
    samples, variants = dosages.shape
    traits = phenotypes.shape[1]
    nz = n // 4
    block = traits // n
    w = WIDTH
    chunks = variants // w
    g = -(-share // 16) * 16
    f32 = jnp.float32
    vm = pltpu.VMEM
    dma = pltpu.SemaphoreType.DMA
    nq = max(npos - 1, 1)
    scratch = [
        vm((samples, variants), jnp.bfloat16),
        vm((samples, traits), jnp.bfloat16),
        vm((chunks - 2, 2, 2, nz, w, block), f32),
        vm((chunks - 2, 2, nz, w, block), f32),
        vm((chunks - 2, nz, w, block), f32),
        vm((chunks - 2, nz - 1, w, block), f32),
        vm((2, nz, 2, 2, w, block), f32),
        vm((2, nz - 1, 2, 2, w, block), f32),
        vm((2, 2, w, block), f32),
        vm((2, w, block), f32),
        vm((w, samples), jnp.bfloat16),
        vm((2, 2, nz, g + 8, block), f32),
        vm((2, nz, g + 8, block), f32),
        vm((nz, g + 8, block), f32),
        vm((nz - 1, g + 8, block), f32),
        vm((chunks + g, w), f32),
        vm((chunks + g, w), f32),
        vm((chunks + g, w), f32),
        vm((nz - 1, chunks + g, w), f32),
        vm((npos, share, samples), f32),
        vm((nq, share, samples), f32),
        vm((g, samples), f32),
        dma((2, chunks)), dma((2, chunks)),
        dma((chunks, nz - 1)), dma((chunks, nz - 1)),
        dma((4,)), dma((4,)),
        dma((2, nz - 1)), dma((2, nz - 1)),
        dma((nq,)), dma((nq,)),
        dma((chunks,)), dma((2 * nz,)),
    ]
    flops = 2 * samples * variants * traits
    return pl.pallas_call(
        functools.partial(kernel, nz, npos, share),
        out_shape=(
            jax.ShapeDtypeStruct((chunks, w, block), f32),
            jax.ShapeDtypeStruct((g + 8, block), f32),
            jax.ShapeDtypeStruct((chunks + g, w), f32),
        ),
        in_specs=[pl.BlockSpec(memory_space=pl.ANY)] * 2
        + [pl.BlockSpec(memory_space=pltpu.VMEM)],
        out_specs=[pl.BlockSpec(memory_space=pltpu.VMEM)] * 3,
        scratch_shapes=scratch,
        compiler_params=pltpu.CompilerParams(
            collective_id=0, has_side_effects=True, vmem_limit_bytes=60 * 1024 * 1024
        ),
        cost_estimate=pl.CostEstimate(
            flops=flops, bytes_accessed=2 * samples * (variants + traits), transcendentals=0
        ),
    )(dosages, phenotypes, masked_t)


def per_device(dosages, phenotypes, gene_weights, gene_start, gene_end):
    variants = dosages.shape[1]
    genes = gene_weights.shape[1]
    n, npos = lax.axis_size("samp"), lax.axis_size("pos")
    share = genes // npos
    offset = lax.axis_index("pos") * variants
    position = offset + lax.broadcasted_iota(jnp.int32, (genes, variants), 1)
    inside = (position >= gene_start[:, None]) & (position < gene_end[:, None])
    weights_t = gene_weights.T
    masked_t = jnp.where(inside, weights_t, jnp.zeros_like(weights_t))
    out, extra, sums = reduce_all(dosages, phenotypes, masked_t, n, npos, share)
    samples = dosages.shape[0] * n
    chunks = out.shape[0]
    g = sums.shape[0] - chunks
    mean_dose = sums[:chunks].reshape(-1) / samples
    mean_pred = sums[chunks : chunks + share, 0] / samples
    mean_trait = extra[g] / samples
    marginal = out.reshape(variants, -1).T
    variant_z = marginal / jnp.sqrt(
        samples * (mean_trait[:, None] + EPSILON) * (mean_dose[None, :] + EPSILON)
    )
    gene_z = extra[:share].T / jnp.sqrt(
        samples * (mean_trait[:, None] + EPSILON) * (mean_pred[None, :] + EPSILON)
    )
    return (variant_z, gene_z)


def solution(mesh):
    return jax.shard_map(
        per_device,
        mesh=mesh,
        in_specs=(P("samp", "pos"), P("samp", None), P("pos", None), P(), P()),
        out_specs=(P("samp", "pos"), P("samp", "pos")),
        check_vma=False,
    )
```

```python
import functools

import jax
import jax.numpy as jnp
from jax import lax
from jax.experimental import pallas as pl
from jax.experimental.pallas import tpu as pltpu
from jax.sharding import PartitionSpec as P

EPSILON = 1e-06
WIDTH = 128
MESH = pl.DeviceIdType.MESH


def kernel(
    nz, npos, share, dos_hbm, ph_hbm, wt, out, ex_out, ar_out,
    dos, ph, part, r1, r2, r3, zpart, z1, z2, z3, xt, ex, e1, e2, e3, ar, a1, a2, a3, pp, pr, pf,
    s_sem, v_sem, s3_sem, v3_sem, es_sem, ev_sem, es3_sem, ev3_sem, ps_sem, pv_sem,
    dl_sem, pl_sem,
):
    samples, variants = dos.shape
    traits = ph.shape[1]
    chunks, w, block = variants // WIDTH, WIDTH, out.shape[0]
    tile = 2 * block
    me = lax.axis_index("samp")
    mp = lax.axis_index("pos")
    mx = lax.rem(me, 2)
    my = lax.rem(me // 2, 2)
    mz = me // 4
    xp = (mz * 4 + my * 2 + (1 - mx), mp)
    yp = (mz * 4 + (1 - my) * 2 + mx, mp)

    def zpeer(d):
        return lax.rem(mz + d, nz)

    def zdev(d):
        return (zpeer(d) * 4 + my * 2 + mx, mp)

    def ppeer(d):
        return lax.rem(mp + d, npos)

    def load_dos(c):
        cols = slice(c * w, (c + 1) * w)
        return pltpu.make_async_copy(dos_hbm.at[:, cols], dos.at[:, cols], dl_sem.at[c])

    def load_ph(i):
        cols = pl.ds(pl.multiple_of(i * tile, tile), tile)
        return pltpu.make_async_copy(ph_hbm.at[:, cols], ph.at[:, cols], pl_sem.at[i])

    load_dos(2).start()
    for i in range(2 * nz):
        load_ph(i).start()
    for c in range(chunks):
        if c != 2:
            load_dos(c).start()

    barrier = pltpu.get_barrier_semaphore()
    peers = [xp, yp] + [zdev(d) for d in range(1, nz)]
    peers += [(me, ppeer(d)) for d in range(1, npos)]
    for peer in peers:
        pl.semaphore_signal(barrier, inc=1, device_id=peer, device_id_type=MESH)
    pl.semaphore_wait(barrier, len(peers))

    def remote(src, dst, send, recv, dev):
        return pltpu.make_async_remote_copy(
            src_ref=src, dst_ref=dst, send_sem=send, recv_sem=recv,
            device_id=dev, device_id_type=MESH,
        )

    def order(c):
        return (mx, my, xp, yp) if c % 2 == 0 else (my, mx, yp, xp)

    def compute(c, first=False):
        cols = slice(c * w, (c + 1) * w)
        if c < 6:
            load_dos(c).wait()
        xt[...] = dos[:, cols].T

        def body(i, carry):
            if first:
                load_ph(i).wait()
            res = jnp.dot(
                xt[...],
                ph[:, pl.ds(pl.multiple_of(i * tile, tile), tile)],
                preferred_element_type=jnp.float32,
            )
            z, y = i // 2, lax.rem(i, 2)
            for x in range(2):
                val = res[:, x * block : (x + 1) * block]
                a, b = (x, y) if c % 2 == 0 else (y, x)
                if c < 2:
                    zpart[c, z, a, b] = val
                else:
                    part[c - 2, a, b, z] = val
            return carry

        lax.fori_loop(0, 2 * nz, body, 0)

    def copy1(c):
        f, _, dev, _ = order(c)
        return remote(part.at[c - 2, 1 - f], r1.at[c - 2], s_sem.at[0, c], v_sem.at[0, c], dev)

    def copy2(c):
        f, s, _, dev = order(c)
        return remote(part.at[c - 2, f, 1 - s], r2.at[c - 2], s_sem.at[1, c], v_sem.at[1, c], dev)

    def copy3(c, d):
        f, s, _, _ = order(c)
        return remote(
            part.at[c - 2, f, s, zpeer(d)], r3.at[c - 2, d - 1],
            s3_sem.at[c, d - 1], v3_sem.at[c, d - 1], zdev(d),
        )

    def add1(c, other):
        f, s, _, _ = order(c)
        k = 1 - s if other else s

        def body(z, carry):
            part[c - 2, f, k, z] = part[c - 2, f, k, z] + r1[c - 2, k, z]
            return carry

        lax.fori_loop(0, nz, body, 0)

    def stage2(c):
        copy1(c).wait_recv()
        add1(c, True)
        copy2(c).start()
        add1(c, False)

    def stage3(c):
        f, s, _, _ = order(c)
        copy2(c).wait_recv()

        def body(z, carry):
            part[c - 2, f, s, z] = part[c - 2, f, s, z] + r2[c - 2, z]
            return carry

        lax.fori_loop(0, nz, body, 0)
        for d in range(nz - 1, 0, -1):
            copy3(c, d).start()

    def finish(c):
        f, s, _, _ = order(c)
        total = part[c - 2, f, s, mz]
        for d in range(1, nz):
            copy3(c, d).wait_recv()
            total = total + r3[c - 2, d - 1]
        out[:, c * w : (c + 1) * w] = total.T

    def zcopy1(c, d):
        return remote(
            zpart.at[c, zpeer(d)], z1.at[c, d - 1],
            s3_sem.at[c, d - 1], v3_sem.at[c, d - 1], zdev(d),
        )

    def zcopy2(c):
        f, _, dev, _ = order(c)
        return remote(
            zpart.at[c, mz, 1 - f], z2.at[c], s_sem.at[0, c], v_sem.at[0, c], dev
        )

    def zcopy3(c):
        f, s, _, dev = order(c)
        return remote(
            zpart.at[c, mz, f, 1 - s], z3.at[c], s_sem.at[1, c], v_sem.at[1, c], dev
        )

    def zstage2(c):
        f, _, _, _ = order(c)
        for d in range(1, nz):
            zcopy1(c, d).wait_recv()
        for k in range(2):
            for m in range(2):
                total = zpart[c, mz, k, m]
                for d in range(1, nz):
                    total = total + z1[c, d - 1, k, m]
                zpart[c, mz, k, m] = total
        zcopy2(c).start()

    def zstage3(c):
        f, _, _, _ = order(c)
        zcopy2(c).wait_recv()
        for m in range(2):
            zpart[c, mz, f, m] = zpart[c, mz, f, m] + z2[c, m]
        zcopy3(c).start()

    def zfinish(c):
        f, s, _, _ = order(c)
        zcopy3(c).wait_recv()
        out[:, c * w : (c + 1) * w] = (zpart[c, mz, f, s] + z3[c]).T

    def pcopy(d):
        return remote(
            pp.at[ppeer(d)], pr.at[d - 1], ps_sem.at[d - 1], pv_sem.at[d - 1],
            (me, ppeer(d)),
        )

    def predict():
        step = min(samples, 256)

        def body(i, carry):
            rows = pl.ds(pl.multiple_of(i * step, step), step)
            res = lax.dot_general(
                wt[...], dos[rows, :], (((1,), (1,)), ((), ())),
                preferred_element_type=jnp.float32,
            )
            for q in range(npos):
                pp[q, :, rows] = res[q * share : (q + 1) * share]
            return carry

        lax.fori_loop(0, samples // step, body, 0)
        for d in range(1, npos):
            pcopy(d).start()

    def squares(ref, cols, width):
        step = min(samples, 256)

        def body(i, acc):
            v = ref[pl.ds(pl.multiple_of(i * step, step), step), cols].astype(jnp.float32)
            return acc + jnp.sum(v * v, axis=0, keepdims=True)

        return lax.fori_loop(0, samples // step, body, jnp.zeros((1, width), jnp.float32))

    def dose_squares():
        for c in range(chunks):
            ar[c : c + 1, :] = squares(dos, slice(c * w, (c + 1) * w), w)

    def small():
        pred = pp[mp]
        for d in range(1, npos):
            pcopy(d).wait_recv()
            pred = pred + pr[d - 1]
        pf[...] = jnp.zeros_like(pf)
        pf[0:share, :] = pred
        full = pf[...]
        low = full.astype(jnp.bfloat16)
        ar[chunks : chunks + pf.shape[0], :] = jnp.broadcast_to(
            jnp.sum(full * full, axis=1, keepdims=True), (pf.shape[0], w)
        )
        g = pf.shape[0]

        def body(i, carry):
            cols = pl.ds(pl.multiple_of(i * tile, tile), tile)
            res = jnp.dot(low, ph[:, cols], preferred_element_type=jnp.float32)
            tsq = jnp.broadcast_to(squares(ph, cols, tile), (8, tile))
            z, y = i // 2, lax.rem(i, 2)
            for x in range(2):
                ex[x, y, z, 0:g, :] = res[:, x * block : (x + 1) * block]
                ex[x, y, z, g : g + 8, :] = tsq[:, x * block : (x + 1) * block]
            return carry

        lax.fori_loop(0, 2 * nz, body, 0)

    ecopy1 = remote(ex.at[1 - mx], e1, es_sem.at[0], ev_sem.at[0], xp)
    acopy1 = remote(ar, a1, es_sem.at[1], ev_sem.at[1], xp)
    ecopy2 = remote(ex.at[mx, 1 - my], e2, es_sem.at[2], ev_sem.at[2], yp)
    acopy2 = remote(ar_out, a2, es_sem.at[3], ev_sem.at[3], yp)

    def ecopy3(d):
        return remote(
            ex.at[mx, my, zpeer(d)], e3.at[d - 1],
            es3_sem.at[0, d - 1], ev3_sem.at[0, d - 1], zdev(d),
        )

    def acopy3(d):
        return remote(
            ar, a3.at[d - 1], es3_sem.at[1, d - 1], ev3_sem.at[1, d - 1], zdev(d)
        )

    def small1():
        ecopy1.start()
        acopy1.start()

    def small2():
        ecopy1.wait_recv()
        ex[mx] = ex[mx] + e1[...]
        ecopy2.start()
        acopy1.wait()
        ar_out[...] = ar[...] + a1[...]
        acopy2.start()

    def small3():
        ecopy2.wait_recv()
        ex[mx, my] = ex[mx, my] + e2[...]
        acopy2.wait()
        ar[...] = ar_out[...] + a2[...]
        for d in range(nz - 1, 0, -1):
            ecopy3(d).start()
            acopy3(d).start()

    def small4():
        total = ex[mx, my, mz]
        sums = ar[...]
        for d in range(1, nz):
            ecopy3(d).wait_recv()
            acopy3(d).wait_recv()
            total = total + e3[d - 1]
            sums = sums + a3[d - 1]
        ex_out[...] = total
        ar_out[...] = sums

    pairs = chunks // 2 - 1
    for t in range(max(pairs + 5, 9)):
        if t == 0:
            compute(2, first=True)
            copy1(2).start()
            compute(3)
            copy1(3).start()
            for c in range(2):
                compute(c)
                for d in range(nz - 1, 0, -1):
                    zcopy1(c, d).start()
        if t + 1 < pairs:
            for c in (2 * t + 4, 2 * t + 5):
                compute(c)
                copy1(c).start()
        if 0 <= t < pairs:
            for c in (2 * t + 2, 2 * t + 3):
                stage2(c)
        if t == 0:
            for c in range(chunks):
                if c >= min(6, 2 * pairs + 2):
                    load_dos(c).wait()
            predict()
        if t == 1:
            dose_squares()
        if t == 2:
            small()
            small1()
        if t == 3:
            small2()
        if t == 4:
            small3()
        if 0 <= t - 1 < pairs:
            for c in (2 * t, 2 * t + 1):
                stage3(c)
        if t == pairs:
            zstage2(0)
            zstage2(1)
        if t == pairs + 1:
            zstage3(0)
            zstage3(1)
        if t == 6:
            small4()
        if t == pairs + 2:
            zfinish(0)
            zfinish(1)
        if 0 <= t - 4 < pairs:
            for c in (2 * t - 6, 2 * t - 5):
                finish(c)
    for c in range(2):
        zcopy2(c).wait_send()
        zcopy3(c).wait_send()
        for d in range(1, nz):
            zcopy1(c, d).wait_send()
    for c in range(2, chunks):
        copy1(c).wait_send()
        copy2(c).wait_send()
        for d in range(1, nz):
            copy3(c, d).wait_send()
    ecopy1.wait_send()
    ecopy2.wait_send()
    for d in range(1, nz):
        ecopy3(d).wait_send()
        acopy3(d).wait_send()
    for d in range(1, npos):
        pcopy(d).wait_send()


def reduce_all(dosages, phenotypes, masked_t, n, npos, share):
    samples, variants = dosages.shape
    traits = phenotypes.shape[1]
    nz = n // 4
    block = traits // n
    w = WIDTH
    chunks = variants // w
    g = -(-share // 16) * 16
    f32 = jnp.float32
    vm = pltpu.VMEM
    dma = pltpu.SemaphoreType.DMA
    nq = max(npos - 1, 1)
    scratch = [
        vm((samples, variants), jnp.bfloat16),
        vm((samples, traits), jnp.bfloat16),
        vm((chunks - 2, 2, 2, nz, w, block), f32),
        vm((chunks - 2, 2, nz, w, block), f32),
        vm((chunks - 2, nz, w, block), f32),
        vm((chunks - 2, nz - 1, w, block), f32),
        vm((2, nz, 2, 2, w, block), f32),
        vm((2, nz - 1, 2, 2, w, block), f32),
        vm((2, 2, w, block), f32),
        vm((2, w, block), f32),
        vm((w, samples), jnp.bfloat16),
        vm((2, 2, nz, g + 8, block), f32),
        vm((2, nz, g + 8, block), f32),
        vm((nz, g + 8, block), f32),
        vm((nz - 1, g + 8, block), f32),
        vm((chunks + g, w), f32),
        vm((chunks + g, w), f32),
        vm((chunks + g, w), f32),
        vm((nz - 1, chunks + g, w), f32),
        vm((npos, share, samples), f32),
        vm((nq, share, samples), f32),
        vm((g, samples), f32),
        dma((2, chunks)), dma((2, chunks)),
        dma((chunks, nz - 1)), dma((chunks, nz - 1)),
        dma((4,)), dma((4,)),
        dma((2, nz - 1)), dma((2, nz - 1)),
        dma((nq,)), dma((nq,)),
        dma((chunks,)), dma((2 * nz,)),
    ]
    flops = 2 * samples * variants * traits
    return pl.pallas_call(
        functools.partial(kernel, nz, npos, share),
        out_shape=(
            jax.ShapeDtypeStruct((block, variants), f32),
            jax.ShapeDtypeStruct((g + 8, block), f32),
            jax.ShapeDtypeStruct((chunks + g, w), f32),
        ),
        in_specs=[pl.BlockSpec(memory_space=pl.ANY)] * 2
        + [pl.BlockSpec(memory_space=pltpu.VMEM)],
        out_specs=[pl.BlockSpec(memory_space=pltpu.VMEM)] * 3,
        scratch_shapes=scratch,
        compiler_params=pltpu.CompilerParams(
            collective_id=0, has_side_effects=True, vmem_limit_bytes=60 * 1024 * 1024
        ),
        cost_estimate=pl.CostEstimate(
            flops=flops, bytes_accessed=2 * samples * (variants + traits), transcendentals=0
        ),
    )(dosages, phenotypes, masked_t)


def per_device(dosages, phenotypes, gene_weights, gene_start, gene_end):
    variants = dosages.shape[1]
    genes = gene_weights.shape[1]
    n, npos = lax.axis_size("samp"), lax.axis_size("pos")
    share = genes // npos
    offset = lax.axis_index("pos") * variants
    position = offset + lax.broadcasted_iota(jnp.int32, (genes, variants), 1)
    inside = (position >= gene_start[:, None]) & (position < gene_end[:, None])
    weights_t = gene_weights.T
    masked_t = jnp.where(inside, weights_t, jnp.zeros_like(weights_t))
    out, extra, sums = reduce_all(dosages, phenotypes, masked_t, n, npos, share)
    samples = dosages.shape[0] * n
    chunks = variants // WIDTH
    g = sums.shape[0] - chunks
    mean_dose = sums[:chunks].reshape(-1) / samples
    mean_pred = sums[chunks : chunks + share, 0] / samples
    mean_trait = extra[g] / samples
    marginal = out
    variant_z = marginal / jnp.sqrt(
        samples * (mean_trait[:, None] + EPSILON) * (mean_dose[None, :] + EPSILON)
    )
    gene_z = extra[:share].T / jnp.sqrt(
        samples * (mean_trait[:, None] + EPSILON) * (mean_pred[None, :] + EPSILON)
    )
    return (variant_z, gene_z)


def solution(mesh):
    return jax.shard_map(
        per_device,
        mesh=mesh,
        in_specs=(P("samp", "pos"), P("samp", None), P("pos", None), P(), P()),
        out_specs=(P("samp", "pos"), P("samp", "pos")),
        check_vma=False,
    )
```
